32 devices in a mesh: aux: 4 (over y, x), tile: 8 (over z, core).
Axes of the slice: x: 2, y: 2, z: 4, core: 2. Of those that a mesh axis runs over, the one named last changes fastest.
Arguments:
- integrals: bfloat16 [11904, 2, 2944], P(('aux', 'tile')), may hold values from -0.57421875 to 0.57421875
- coefficients: bfloat16 [2944, 2048], replicated, may hold values from -0.109375 to 0.109375
- owned_tiles: int32 [2, 16], replicated, may hold values from 0 to 15, each once within a row
- pair_list: int32 [2, 16, 4], P(None, 'tile'), may hold values from -1 to 15, as said below
- amplitudes: bfloat16 [2, 16, 4, 128, 128], P(None, 'tile'), may hold values from -0.25 to 0.25
Outputs:
- residual: float32 [2, 16, 128, 128], P(None, 'tile')
The draws below stay inside these ranges and needn't reach their ends.
Inputs may be any that keep to these rules, and one draw needn't show every extreme that they name: `pair_list`: every live entry of slot s is a slot within 2 of s; the live entries of one slot are distinct; -1 marks an entry dropped by screening.
All inputs are finite; a program needn't handle non-finite values.
Results may differ from the reference program's by a relative error of at most 0.00087.
Values may be sent and summed in bfloat16 or wider, within the bound.
No kernel may reach another device: no remote copies, remote signals or barrier semaphores. Data moves between devices by JAX's collectives and lax.ppermute only.
A program may use at most 128 MiB of HBM per device.

```python
import jax
import jax.numpy as jnp
from jax import lax

NAUX = 11904
NAO = 2944
TILE = 128
NVT = 16
NB = 2
NPART = 4
PTD = 2
NV = 2048
PT = 16
NOCC = 2


def draw_pair_list(key, part):
    offsets = 2 * PTD + 1
    keys = jax.random.split(jax.random.fold_in(key, 11), NB * PT)
    perms = jax.vmap(lambda one_key: jax.random.permutation(one_key, offsets))(keys)
    picked = perms[:, :NPART].reshape(NB, PT, NPART).astype(jnp.int32) - PTD
    slots = jnp.arange(PT, dtype=jnp.int32)[None, :, None]
    target = slots + picked
    dropped = jax.random.randint(jax.random.fold_in(key, 23), (NB, PT, NPART), 0, 4) == 0
    valid = (target >= 0) & (target < PT) & jnp.logical_not(dropped)
    return jnp.where(valid, target, -1).astype(jnp.int32)


def block_scale(key, shape, pieces, low, top_value):
    def one(dim, parts):
        heights = jax.random.uniform(jax.random.fold_in(jax.random.fold_in(key, 6), dim), (parts,), jnp.float32, low / len(pieces), top_value / len(pieces))
        return jnp.repeat(jnp.exp(heights), shape[dim] // parts).reshape((-1,) + (1,) * (len(shape) - dim - 1))

    loudness = one(*pieces[0])
    for cut in pieces[1:]:
        loudness = loudness * one(*cut)
    return loudness


def centred(rng, extent, deviation, most, cuts=(), held_as=jnp.bfloat16):
    values = jax.random.normal(rng, extent, jnp.float32) * deviation
    if len(cuts) > 0:
        values = block_scale(rng, extent, cuts, -0.22, 0.18) * values
    return jnp.clip(values, min=-most, max=most).astype(held_as)


def setup_inputs(seed: int = 0) -> dict:
    key_list = jax.random.split(jax.random.key(seed), 6)
    return {
        "integrals": centred(key_list[0], (NAUX, NOCC, NAO), (NAUX ** -0.25), 0.57421875, ((0, 32),)),
        "coefficients": centred(key_list[1], (NAO, NV), NAO ** -0.5, 0.109375),
        "owned_tiles": jax.vmap(lambda own: jax.random.permutation(own, PT))(jax.random.split(key_list[2], NB)).reshape((NB, PT)).astype(jnp.int32),
        "pair_list": draw_pair_list(jax.random.fold_in(key_list[5], 71), 0),
        "amplitudes": centred(key_list[4], (NB, PT, NPART, TILE, TILE), (TILE * NPART) ** -0.5, 0.25, ((1, 8),)),
    }


def reference(integrals, coefficients, owned_tiles, pair_list, amplitudes):
    occ_batch = integrals.shape[1] // NB
    results = []
    for occ_group in range(NB):
        int_block = integrals[:, occ_group * occ_batch:(occ_group + 1) * occ_batch, :].reshape(NAUX * occ_batch, NAO)
        half_done = jnp.dot(int_block, coefficients, preferred_element_type=jnp.float32).astype(jnp.bfloat16)
        half_done = half_done.reshape(NAUX, occ_batch * NVT, TILE)
        ordered = jnp.take(half_done, owned_tiles[occ_group], axis=1)

        def one_slot(slot_idx):
            mine = lax.dynamic_index_in_dim(ordered, slot_idx, 1, keepdims=False).astype(jnp.float32)
            listed = pair_list[occ_group, slot_idx]
            live_mask = (listed >= 0).astype(jnp.float32)
            others = jnp.take(ordered, jnp.maximum(listed, 0), axis=1).astype(jnp.float32)
            pair_ints = jnp.einsum("qa,qkb->kab", mine, others, precision=lax.Precision.HIGHEST)
            pair_ints = pair_ints * live_mask[:, None, None]
            amp_tiles = amplitudes[occ_group, slot_idx].astype(jnp.float32)
            return jnp.einsum("kab,kbc->ac", pair_ints, amp_tiles, precision=lax.Precision.HIGHEST)

        results.append(lax.map(one_slot, jnp.arange(PT, dtype=jnp.int32)))
    return jnp.stack(results)
```

```python
import functools

import jax
import jax.numpy as jnp
from jax import lax
from jax.experimental import pallas as pl
from jax.experimental.pallas import tpu as pltpu
from jax.sharding import PartitionSpec as P

NB = 2
BAND = 5
AXES = ("aux", "tile")
VMEM = pl.BlockSpec(memory_space=pltpu.VMEM)
SMEM = pl.BlockSpec(memory_space=pltpu.SMEM)
PARAMS = pltpu.CompilerParams(vmem_limit_bytes=56 * 2**20)
F32, BF16 = jnp.float32, jnp.bfloat16


def shape(dims, dtype):
    return jax.ShapeDtypeStruct(tuple(dims), dtype)


def place():
    t = lax.axis_index("tile")
    return lax.axis_index("aux"), t // 2, t % 2


def chip_slot(a, batch):
    return 2 * ((a % 2) ^ batch) + a // 2


def pack_kernel(pairs, amps, zmsg, mine, other, *, npart, width):
    a, z, c = place()
    per_dev = amps.shape[1]
    first = lax.axis_index("tile") * per_dev

    def pack(batch, s, dst):
        offsets, live, seen = [], [], [jnp.int32(0)] * BAND
        for k in range(npart):
            p = pairs[batch, s, k]
            o = p - (first + s) + BAND // 2
            ok = p >= 0
            offsets.append(o)
            live.append(ok)
            for n in range(BAND):
                seen[n] = jnp.where(ok & (o == n), 1, seen[n])
        m = jnp.int32(BAND - 1)
        for n in reversed(range(BAND)):
            m = jnp.where(seen[n] == 0, n, m)
        for j in range(npart):
            want = j + jnp.where(j >= m, 1, 0)
            found, at = jnp.int32(0), jnp.int32(0)
            for k in range(npart):
                hit = live[k] & (offsets[k] == want)
                found = jnp.where(hit, 1, found)
                at = jnp.where(hit, k, at)
            block = amps[batch, s, at]
            dst[pl.ds(j * width, width), :] = jnp.where(found == 1, block, jnp.zeros_like(block))
        code = jnp.full((16, width), m.astype(F32), F32)
        dst[pl.ds(npart * width, 16), :] = code.astype(BF16)

    pack(c ^ (a % 2), a // 2, zmsg)
    for s in range(per_dev):
        pack(c, s, mine.at[s])
        pack(1 - c, s, other.at[s])


def half_kernel(x_ref, c_ref, mine, other, acc, *, batch_occ):
    core = lax.axis_index("tile") % 2
    rows, occ, ao = x_ref.shape
    cols = c_ref.shape[1]
    padded = mine.shape[1]
    prod = jnp.dot(x_ref[...].reshape(rows * occ, ao), c_ref[...], preferred_element_type=F32)
    for n in range(cols // 128):
        acc[n] = prod[:, n * 128 : (n + 1) * 128]
    for i in range(batch_occ):
        for n in range(cols // 128):
            lanes = slice(n * 128, (n + 1) * 128)
            for dst, b in ((mine, core), (other, 1 - core)):
                part = acc[n, pl.ds(b * batch_occ + i, rows, stride=occ), :]
                dst[i, :rows, lanes] = part.astype(BF16)
    for dst in (mine, other):
        dst[:, rows:, :] = jnp.zeros((batch_occ, padded - rows, cols), BF16)


def pair_kernel(owned, y_mine, y_other, out, *, width, step_slots):
    core = lax.axis_index("tile") % 2
    slots = owned.shape[1]
    virt_tiles = y_mine.shape[2] // width
    first = pl.program_id(0) * step_slots

    def tile(ref, s):
        ident = owned[core, jnp.clip(s, 0, slots - 1)]
        col = pl.multiple_of(ident % virt_tiles * width, width)
        return ref[ident // virt_tiles, :, pl.ds(col, width)]

    reach = BAND // 2
    for t in range(0, step_slots, 2):
        total = None
        for ref in (y_mine, y_other):
            tiles = [tile(ref, first + t + n) for n in range(-reach, 2 + reach)]
            left = jnp.concatenate(tiles[reach : reach + 2], axis=1)
            right = jnp.concatenate(tiles, axis=1)
            part = lax.dot_general(left, right, (((0,), (0,)), ((), ())), preferred_element_type=F32)
            total = part if total is None else total + part
        for u in range(2):
            for o in range(BAND):
                out[t + u, o] = total[u * width : (u + 1) * width, (u + o) * width : (u + o + 1) * width]


def residual_kernel(*refs, aux_count, chips, npart, width):
    a, z, c = place()
    ints, mine, other = refs[:3]
    far = refs[3 : 3 + (chips - 1) * aux_count]
    outs = refs[3 + (chips - 1) * aux_count :]
    per_chip = aux_count

    def residual(slot, amp):
        rows = amp[: npart * width]
        m = amp[npart * width :].astype(F32)[:1, :]
        picked = [
            jnp.where(m > j, ints[slot, j], ints[slot, j + 1]) for j in range(npart)
        ]
        picked = jnp.concatenate(picked, axis=1)
        high = picked.astype(BF16)
        low = (picked - high.astype(F32)).astype(BF16)
        return jnp.dot(high, rows, preferred_element_type=F32) + jnp.dot(
            low, rows, preferred_element_type=F32
        )

    for e in range(aux_count):
        peer = a ^ e
        at = peer // 2
        own = jnp.where(peer % 2 == 0, mine[at], other[at])
        outs[e][0] = residual(per_chip * z + chip_slot(peer, c), own)
        for d in range(1, chips):
            amp = far[(d - 1) * aux_count + e][...]
            outs[e][d] = residual(per_chip * (z ^ d) + chip_slot(peer, c), amp)


def sum_split_kernel(*refs, count):
    ins, outs = refs[:count], refs[count:]
    for d, out in enumerate(outs):
        total = ins[0][d]
        for ref in ins[1:]:
            total = total + ref[d]
        out[...] = total


def sum_kernel(*refs):
    total = refs[0][...]
    for ref in refs[1:-1]:
        total = total + ref[...]
    refs[-1][...] = total


def place_kernel(*refs):
    a, _, c = place()
    out = refs[-1]
    for j, ref in enumerate(refs[:-1]):
        src = a ^ j
        out[(src % 2) ^ c, src // 2] = ref[...]


def call(kernel, outs, count, params=PARAMS, **kw):
    return pl.pallas_call(
        kernel, in_specs=[VMEM] * count, out_specs=jax.tree.map(lambda _: VMEM, outs), out_shape=outs,
        compiler_params=params, **kw,
    )


def per_device(integrals, coefficients, owned_tiles, pair_list, amplitudes):
    aux_count, tile_count = lax.axis_size("aux"), lax.axis_size("tile")
    chips = tile_count // 2
    rows, occ, ao = integrals.shape
    virt = coefficients.shape[1]
    batch_occ = occ // NB
    _, per_dev, npart, width, _ = amplitudes.shape
    slots = owned_tiles.shape[1]
    assert aux_count == 2 * per_dev and per_dev == 2

    def exchange(x, target):
        perm = []
        for a in range(aux_count):
            for z in range(chips):
                for c in range(2):
                    a2, z2, c2 = target(a, z, c)
                    perm.append((a * tile_count + 2 * z + c, a2 * tile_count + 2 * z2 + c2))
        return lax.ppermute(x, AXES, perm)

    msg_rows = npart * width + 16
    msg = shape((msg_rows, width), BF16)
    pair = shape((per_dev, msg_rows, width), BF16)
    zmsg, mine, other = pl.pallas_call(
        functools.partial(pack_kernel, npart=npart, width=width),
        in_specs=[SMEM, VMEM], out_specs=[VMEM] * 3, out_shape=[msg, pair, pair], compiler_params=PARAMS,
    )(pair_list, amplitudes)
    along = [
        exchange(zmsg, lambda a, z, c, d=d: (a, z ^ d, c ^ (a % 2))) for d in range(1, chips)
    ]
    other = exchange(other, lambda a, z, c: (a, z, 1 - c))
    far = []
    for got in along:
        far.append(got)
        for e in range(1, aux_count):
            far.append(exchange(got, lambda a, z, c, e=e: (a ^ e, z, c)))

    block = 512
    padded = -(-rows // 16) * 16
    half = shape((batch_occ, padded, virt), BF16)
    half_spec = pl.BlockSpec((batch_occ, padded, block), lambda n: (0, 0, n))
    y_mine, y_send = pl.pallas_call(
        functools.partial(half_kernel, batch_occ=batch_occ),
        grid=(virt // block,),
        in_specs=[pl.BlockSpec((rows, occ, ao), lambda n: (0, 0, 0)), pl.BlockSpec((ao, block), lambda n: (0, n))],
        out_specs=[half_spec, half_spec],
        out_shape=[half, half],
        scratch_shapes=[pltpu.VMEM((block // 128, rows * occ, 128), F32)],
        compiler_params=PARAMS,
        cost_estimate=pl.CostEstimate(
            flops=2 * rows * occ * ao * virt, bytes_accessed=2 * (rows * occ * ao + ao * virt), transcendentals=0
        ),
    )(integrals, coefficients)
    y_other = exchange(y_send, lambda a, z, c: (a, z, 1 - c))

    step_slots = 16
    pair_ints = pl.pallas_call(
        functools.partial(pair_kernel, width=width, step_slots=step_slots),
        grid=(slots // step_slots,),
        in_specs=[SMEM, VMEM, VMEM],
        out_specs=pl.BlockSpec((step_slots, BAND, width, width), lambda n: (n, 0, 0, 0)),
        out_shape=shape((slots, BAND, width, width), F32),
        compiler_params=PARAMS,
    )(owned_tiles, y_mine, y_other)

    shares = call(
        functools.partial(residual_kernel, aux_count=aux_count, chips=chips, npart=npart, width=width),
        [shape((chips, width, width), F32)] * aux_count, 3 + len(far),
    )(pair_ints, mine, other, *far)

    got = [shares[0]]
    for e in range(1, aux_count):
        got.append(exchange(shares[e], lambda a, z, c, e=e: (a ^ e, z, c)))
    sums = call(
        functools.partial(sum_split_kernel, count=aux_count), [shape((width, width), F32)] * chips, aux_count
    )(*got)
    got = [sums[0]] + [exchange(sums[d], lambda a, z, c, d=d: (a, z ^ d, c)) for d in range(1, chips)]
    done = call(sum_kernel, shape((width, width), F32), chips)(*got)
    got = [exchange(done, lambda a, z, c, j=j: (a ^ j, z, (a % 2) ^ c)) for j in range(aux_count)]
    return call(place_kernel, shape((NB, per_dev, width, width), F32), aux_count)(*got)


def solution(mesh):
    in_specs = (
        P(("aux", "tile"), None, None),
        P(),
        P(),
        P(None, "tile", None),
        P(None, "tile", None, None, None),
    )
    out_specs = P(None, "tile", None, None)
    return jax.shard_map(
        per_device, mesh=mesh, in_specs=in_specs, out_specs=out_specs, check_vma=False
    )
```

```python
import functools

import jax
import jax.numpy as jnp
from jax import lax
from jax.experimental import pallas as pl
from jax.experimental.pallas import tpu as pltpu
from jax.sharding import PartitionSpec as P

NB = 2
BAND = 5
REACH = BAND // 2
HALF_FLOPS = 10**9
MIB = 2**20
AXES = ("aux", "tile")
VMEM = pl.BlockSpec(memory_space=pltpu.VMEM)
SMEM = pl.BlockSpec(memory_space=pltpu.SMEM)
ANY = pl.BlockSpec(memory_space=pl.ANY)
HBM = pl.BlockSpec(memory_space=pltpu.HBM)
F32, BF16 = jnp.float32, jnp.bfloat16


def shape(dims, dtype):
    return jax.ShapeDtypeStruct(tuple(dims), dtype)


def place():
    t = lax.axis_index("tile")
    return lax.axis_index("aux"), t // 2, t % 2


def chip_slot(a, batch):
    return 2 * ((a % 2) ^ batch) + a // 2


def call(kernel, outs, specs, limit, flops=10**6, **kw):
    return pl.pallas_call(
        kernel, in_specs=specs, out_specs=jax.tree.map(lambda _: VMEM, outs), out_shape=outs,
        compiler_params=pltpu.CompilerParams(vmem_limit_bytes=limit * MIB),
        cost_estimate=pl.CostEstimate(flops=flops, bytes_accessed=10**5, transcendentals=0), **kw,
    )


def pack_kernel(pairs, amps, zmsg, mine, other, *, npart, width):
    a, z, c = place()
    per_dev = amps.shape[1]
    first = lax.axis_index("tile") * per_dev

    def pack(batch, s, dst):
        offsets, live, seen = [], [], [jnp.int32(0)] * BAND
        for k in range(npart):
            p = pairs[batch, s, k]
            o = p - (first + s) + REACH
            ok = p >= 0
            offsets.append(o)
            live.append(ok)
            for n in range(BAND):
                seen[n] = jnp.where(ok & (o == n), 1, seen[n])
        m = jnp.int32(BAND - 1)
        for n in reversed(range(BAND)):
            m = jnp.where(seen[n] == 0, n, m)
        for j in range(npart):
            want = j + jnp.where(j >= m, 1, 0)
            found, at = jnp.int32(0), jnp.int32(0)
            for k in range(npart):
                hit = live[k] & (offsets[k] == want)
                found = jnp.where(hit, 1, found)
                at = jnp.where(hit, k, at)
            block = amps[batch, s, at]
            dst[pl.ds(j * width, width), :] = jnp.where(found == 1, block, jnp.zeros_like(block))
        code = jnp.full((16, width), m.astype(F32), F32)
        dst[pl.ds(npart * width, 16), :] = code.astype(BF16)

    pack(c ^ (a % 2), a // 2, zmsg)
    for s in range(per_dev):
        pack(c, s, mine.at[s])
        pack(1 - c, s, other.at[s])


def half_columns(x_ref, c_ref, start, mine, other, acc, batch_occ):
    core = lax.axis_index("tile") % 2
    rows, occ, ao = x_ref.shape
    cols = mine.shape[2]
    padded = mine.shape[1]
    prod = jnp.dot(
        x_ref[...].reshape(rows * occ, ao), c_ref[:, start : start + cols], preferred_element_type=F32
    )
    for n in range(cols // 128):
        acc[n] = prod[:, n * 128 : (n + 1) * 128]
    for i in range(batch_occ):
        for n in range(cols // 128):
            lanes = slice(n * 128, (n + 1) * 128)
            for dst, b in ((mine, core), (other, 1 - core)):
                part = acc[n, pl.ds(b * batch_occ + i, rows, stride=occ), :]
                dst[i, :rows, lanes] = part.astype(BF16)
    for dst in (mine, other):
        dst[:, rows:, :] = jnp.zeros((batch_occ, padded - rows, cols), BF16)


def first_half_kernel(x_ref, c_hbm, _, mine, other, c_ref, acc, sems, *, batch_occ):
    cols = mine.shape[2]
    parts = c_ref.shape[1] // cols
    get_c = [
        pltpu.make_async_copy(
            c_hbm.at[:, pl.ds(n * cols, cols)], c_ref.at[:, pl.ds(n * cols, cols)], sems.at[n]
        )
        for n in range(parts)
    ]
    for copy in get_c:
        copy.start()
    get_c[0].wait()
    half_columns(x_ref, c_ref, 0, mine, other, acc, batch_occ)
    for copy in get_c[1:]:
        copy.wait()


def half_kernel(x_ref, c_ref, *rest, batch_occ, start):
    mine, other, acc = rest[-3:]
    half_columns(x_ref, c_ref, start, mine, other, acc, batch_occ)


def pair_kernel(owned, *refs, parts, width):
    core = lax.axis_index("tile") % 2
    slots = owned.shape[1]
    y_mine, y_other, (out, tiles, place_of) = refs[:parts], refs[parts : 2 * parts], refs[2 * parts :]
    batch_occ, padded, cols = y_mine[0].shape
    for s in range(slots):
        place_of[owned[core, s]] = s + REACH
    for n in (0, 1, slots + REACH, slots + REACH + 1):
        tiles[:, n * width : (n + 1) * width] = jnp.zeros((2 * padded, width), BF16)
    for i in range(batch_occ):
        for h in range(parts):
            for n in range(cols // width):
                ident = (i * parts + h) * (cols // width) + n
                lanes = pl.ds(pl.multiple_of(place_of[ident] * width, width), width)
                for src, group in enumerate((y_mine, y_other)):
                    rows = slice(src * padded, (src + 1) * padded)
                    tiles[rows, lanes] = group[h][i, :, n * width : (n + 1) * width]
    for t in range(0, slots, 2):
        left = tiles[:, (t + REACH) * width : (t + REACH + 2) * width]
        right = tiles[:, t * width : (t + 2 + 2 * REACH) * width]
        total = lax.dot_general(left, right, (((0,), (0,)), ((), ())), preferred_element_type=F32)
        for u in range(2):
            for o in range(BAND):
                out[t + u, o] = total[u * width : (u + 1) * width, (u + o) * width : (u + o + 1) * width]


def partial_residual(ints, slot, amp, npart, width):
    rows = amp[: npart * width]
    m = amp[npart * width :].astype(F32)[:1, :]
    picked = [jnp.where(m > j, ints[slot, j], ints[slot, j + 1]) for j in range(npart)]
    picked = jnp.concatenate(picked, axis=1)
    high = picked.astype(BF16)
    low = (picked - high.astype(F32)).astype(BF16)
    return jnp.dot(high, rows, preferred_element_type=F32) + jnp.dot(low, rows, preferred_element_type=F32)


def own_kernel(ints, mine, other, out, *, aux_count, npart, width):
    _, z, c = place()
    per_dev = mine.shape[0]
    for s in range(per_dev):
        for src, core in ((mine, c), (other, 1 - c)):
            at = per_dev * core + s
            out[at] = partial_residual(ints, aux_count * z + at, src[s], npart, width)


def far_kernel(ints, *refs, aux_count, distances, npart, width):
    a, z, c = place()
    outs = refs[aux_count:]
    for n, d in enumerate(distances):
        for e in range(aux_count):
            at = chip_slot(a ^ e, c)
            outs[n][at] = partial_residual(ints, aux_count * (z ^ d) + at, refs[e][n], npart, width)


def join_kernel(*refs):
    *ins, _, out = refs
    for n, ref in enumerate(ins):
        out[n] = ref[...]


def sum_kernel(*refs):
    total = refs[0][...]
    for ref in refs[1:-1]:
        total = total + ref[...]
    refs[-1][...] = total


def sum_split_kernel(*refs):
    *ins, keep, give = refs
    core = lax.axis_index("tile") % 2
    per_dev = keep.shape[0]
    for s in range(per_dev):
        for dst, owner in ((keep, core), (give, 1 - core)):
            total = ins[0][per_dev * owner + s]
            for ref in ins[1:]:
                total = total + ref[per_dev * owner + s]
            dst[s] = total


def place_kernel(keep, got, out):
    core = lax.axis_index("tile") % 2
    out[core] = keep[...]
    out[1 - core] = got[...]


def per_device(integrals, coefficients, owned_tiles, pair_list, amplitudes):
    aux_count, tile_count = lax.axis_size("aux"), lax.axis_size("tile")
    chips = tile_count // 2
    rows, occ, ao = integrals.shape
    virt = coefficients.shape[1]
    batch_occ = occ // NB
    _, per_dev, npart, width, _ = amplitudes.shape
    slots = owned_tiles.shape[1]
    assert aux_count == 2 * per_dev and per_dev == 2

    def exchange(x, target):
        perm = []
        for a in range(aux_count):
            for z in range(chips):
                for c in range(2):
                    a2, z2, c2 = target(a, z, c)
                    perm.append((a * tile_count + 2 * z + c, a2 * tile_count + 2 * z2 + c2))
        return lax.ppermute(x, AXES, perm)

    def swap(x):
        return exchange(x, lambda a, z, c: (a, z, 1 - c))

    def round_plane(x):
        return [exchange(x, lambda a, z, c, e=e: (a ^ e, z, c)) for e in range(1, aux_count)]

    parts = 4
    cols = virt // parts
    padded = -(-rows // 16) * 16

    msg_rows = npart * width + 16
    msg = shape((msg_rows, width), BF16)
    pair = shape((per_dev, msg_rows, width), BF16)
    zmsg, mine, other = call(
        functools.partial(pack_kernel, npart=npart, width=width), [msg, pair, pair], [SMEM, VMEM], 12,
            )(pair_list, amplitudes)
    along = [exchange(zmsg, lambda a, z, c, d=d: (a, z ^ d, c ^ (a % 2))) for d in range(1, chips)]
    other = swap(other)
    batches = [range(1, chips - 1), range(chips - 1, chips)]
    far = []

    half = shape((batch_occ, padded, cols), BF16)
    acc = pltpu.VMEM((cols // 128, rows * occ, 128), F32)
    y_mine, y_other = [], []
    after = [zmsg]
    for n in range(parts):
        if n == 0:
            got, send, c = call(
                functools.partial(first_half_kernel, batch_occ=batch_occ),
                [half, half, shape(coefficients.shape, BF16)],
                [VMEM, HBM, ANY], 28, flops=HALF_FLOPS, scratch_shapes=[acc, pltpu.SemaphoreType.DMA((parts,))],
            )(integrals, coefficients, *after)
        else:
            got, send = call(
                functools.partial(half_kernel, batch_occ=batch_occ, start=n * cols),
                [half, half], [VMEM, VMEM] + [ANY] * len(after), 12, flops=HALF_FLOPS, scratch_shapes=[acc],
            )(integrals, c, *after)
        y_mine.append(got)
        y_other.append(swap(send))
        after = [got]
        if n == 2:
            after = far[0][1:]
        if n < len(batches):
            distances = batches[n]
            joined = call(
                join_kernel, shape((len(distances), msg_rows, width), BF16), [VMEM] * len(distances) + [ANY], 12
            )(*[along[d - 1] for d in distances], got)
            far.append([joined] + round_plane(joined))
            after = [joined]

    ints_shape = shape((slots, BAND, width, width), F32)
    tiles_shape = (2 * padded, (slots + BAND - 1) * width)
    ints = call(
        functools.partial(pair_kernel, parts=parts, width=width), ints_shape, [SMEM] + [VMEM] * (2 * parts),
        8 + 4 * slots * BAND * width * width // MIB + 2 * tiles_shape[0] * tiles_shape[1] // MIB,
        scratch_shapes=[pltpu.VMEM(tiles_shape, BF16), pltpu.SMEM((slots,), jnp.int32)],
    )(owned_tiles, *y_mine, *y_other)

    chip_part = shape((aux_count, width, width), F32)
    sizes = dict(aux_count=aux_count, npart=npart, width=width)
    got = [call(functools.partial(own_kernel, **sizes), chip_part, [VMEM] * 3, 12)(ints, mine, other)]
    for distances, amps in zip(batches, far):
        shares = call(
            functools.partial(far_kernel, distances=distances, **sizes),
            [chip_part] * len(distances), [VMEM] * (1 + aux_count), 16,
        )(ints, *amps)
        got += [exchange(share, lambda a, z, c, d=d: (a, z ^ d, c)) for d, share in zip(distances, shares)]
    column = call(sum_kernel, chip_part, [VMEM] * chips, 12)(*got)

    core_part = shape((per_dev, width, width), F32)
    keep, give = call(sum_split_kernel, [core_part] * 2, [VMEM] * aux_count, 12)(column, *round_plane(column))
    return call(place_kernel, shape((NB, per_dev, width, width), F32), [VMEM] * 2, 8)(keep, swap(give))


def solution(mesh):
    in_specs = (
        P(("aux", "tile"), None, None),
        P(),
        P(),
        P(None, "tile", None),
        P(None, "tile", None, None, None),
    )
    out_specs = P(None, "tile", None, None)
    return jax.shard_map(
        per_device, mesh=mesh, in_specs=in_specs, out_specs=out_specs, check_vma=False
    )
```

```python
import functools

import jax
import jax.numpy as jnp
from jax import lax
from jax.experimental import pallas as pl
from jax.experimental.pallas import tpu as pltpu
from jax.sharding import PartitionSpec as P

NB = 2
BAND = 5
REACH = BAND // 2
HALF_FLOPS = 10**9
MIB = 2**20
AXES = ("aux", "tile")
VMEM = pl.BlockSpec(memory_space=pltpu.VMEM)
SMEM = pl.BlockSpec(memory_space=pltpu.SMEM)
ANY = pl.BlockSpec(memory_space=pl.ANY)
HBM = pl.BlockSpec(memory_space=pltpu.HBM)
F32, BF16, F16 = jnp.float32, jnp.bfloat16, jnp.float16
TOP = 15.0


def shape(dims, dtype):
    return jax.ShapeDtypeStruct(tuple(dims), dtype)


def place():
    t = lax.axis_index("tile")
    return lax.axis_index("aux"), t // 2, t % 2


def chip_slot(a, batch):
    return 2 * ((a % 2) ^ batch) + a // 2


def call(kernel, outs, specs, limit, flops=10**6, **kw):
    return pl.pallas_call(
        kernel, in_specs=specs, out_specs=jax.tree.map(lambda _: VMEM, outs), out_shape=outs,
        compiler_params=pltpu.CompilerParams(vmem_limit_bytes=limit * MIB),
        cost_estimate=pl.CostEstimate(flops=flops, bytes_accessed=10**5, transcendentals=0), **kw,
    )


def pack_kernel(pairs, amps, zmsg, mine, other, *, npart, width):
    a, z, c = place()
    per_dev = amps.shape[1]
    first = lax.axis_index("tile") * per_dev

    def pack(batch, s, dst):
        offsets, live, seen = [], [], [jnp.int32(0)] * BAND
        for k in range(npart):
            p = pairs[batch, s, k]
            o = p - (first + s) + REACH
            ok = p >= 0
            offsets.append(o)
            live.append(ok)
            for n in range(BAND):
                seen[n] = jnp.where(ok & (o == n), 1, seen[n])
        m = jnp.int32(BAND - 1)
        for n in reversed(range(BAND)):
            m = jnp.where(seen[n] == 0, n, m)
        for j in range(npart):
            want = j + jnp.where(j >= m, 1, 0)
            found, at = jnp.int32(0), jnp.int32(0)
            for k in range(npart):
                hit = live[k] & (offsets[k] == want)
                found = jnp.where(hit, 1, found)
                at = jnp.where(hit, k, at)
            block = amps[batch, s, at]
            dst[pl.ds(j * width, width), :] = jnp.where(found == 1, block, jnp.zeros_like(block))
        code = jnp.full((16, width), m.astype(F32), F32)
        dst[pl.ds(npart * width, 16), :] = code.astype(BF16)

    pack(c ^ (a % 2), a // 2, zmsg)
    for s in range(per_dev):
        pack(c, s, mine.at[s])
        pack(1 - c, s, other.at[s])


def half_columns(x_ref, c_ref, start, mine, other, acc, batch_occ):
    core = lax.axis_index("tile") % 2
    rows, occ, ao = x_ref.shape
    cols = mine.shape[2]
    padded = mine.shape[1]
    prod = jnp.dot(
        x_ref[...].reshape(rows * occ, ao), c_ref[:, start : start + cols], preferred_element_type=F32
    )
    for n in range(cols // 128):
        acc[n] = prod[:, n * 128 : (n + 1) * 128]
    for i in range(batch_occ):
        for n in range(cols // 128):
            lanes = slice(n * 128, (n + 1) * 128)
            for dst, b in ((mine, core), (other, 1 - core)):
                part = acc[n, pl.ds(b * batch_occ + i, rows, stride=occ), :]
                dst[i, :rows, lanes] = part.astype(BF16)
    for dst in (mine, other):
        dst[:, rows:, :] = jnp.zeros((batch_occ, padded - rows, cols), BF16)


def first_half_kernel(x_ref, c_hbm, _, mine, other, c_ref, acc, sems, *, batch_occ):
    cols = mine.shape[2]
    parts = c_ref.shape[1] // cols
    get_c = [
        pltpu.make_async_copy(
            c_hbm.at[:, pl.ds(n * cols, cols)], c_ref.at[:, pl.ds(n * cols, cols)], sems.at[n]
        )
        for n in range(parts)
    ]
    for copy in get_c:
        copy.start()
    get_c[0].wait()
    half_columns(x_ref, c_ref, 0, mine, other, acc, batch_occ)
    for copy in get_c[1:]:
        copy.wait()


def half_kernel(x_ref, c_ref, *rest, batch_occ, start):
    mine, other, acc = rest[-3:]
    half_columns(x_ref, c_ref, start, mine, other, acc, batch_occ)


def pair_kernel(owned, *refs, parts, width):
    core = lax.axis_index("tile") % 2
    slots = owned.shape[1]
    y_mine, y_other, (out, tiles, place_of) = refs[:parts], refs[parts : 2 * parts], refs[2 * parts :]
    batch_occ, padded, cols = y_mine[0].shape
    for s in range(slots):
        place_of[owned[core, s]] = s + REACH
    for n in (0, 1, slots + REACH, slots + REACH + 1):
        tiles[:, n * width : (n + 1) * width] = jnp.zeros((2 * padded, width), BF16)
    for i in range(batch_occ):
        for h in range(parts):
            for n in range(cols // width):
                ident = (i * parts + h) * (cols // width) + n
                lanes = pl.ds(pl.multiple_of(place_of[ident] * width, width), width)
                for src, group in enumerate((y_mine, y_other)):
                    rows = slice(src * padded, (src + 1) * padded)
                    tiles[rows, lanes] = group[h][i, :, n * width : (n + 1) * width]
    for t in range(0, slots, 2):
        left = tiles[:, (t + REACH) * width : (t + REACH + 2) * width]
        right = tiles[:, t * width : (t + 2 + 2 * REACH) * width]
        total = lax.dot_general(left, right, (((0,), (0,)), ((), ())), preferred_element_type=F32)
        for u in range(2):
            for o in range(BAND):
                out[t + u, o] = total[u * width : (u + 1) * width, (u + o) * width : (u + o + 1) * width]


def partial_residual(ints, slot, amp, npart, width):
    rows = amp[: npart * width]
    m = amp[npart * width :].astype(F32)[:1, :]
    picked = [jnp.where(m > j, ints[slot, j], ints[slot, j + 1]) for j in range(npart)]
    picked = jnp.concatenate(picked, axis=1)
    high = picked.astype(BF16)
    low = (picked - high.astype(F32)).astype(BF16)
    return jnp.dot(high, rows, preferred_element_type=F32) + jnp.dot(low, rows, preferred_element_type=F32)


def encode(blocks, out):
    count, width, _ = blocks.shape
    at = lax.broadcasted_iota(jnp.int32, (16, width), 0)
    codes = jnp.zeros((16, width), F32)
    for n in range(count):
        block = blocks[n]
        peak = jnp.max(jnp.abs(block), axis=0, keepdims=True)
        peak = jnp.max(peak, axis=1, keepdims=True)
        power = jnp.ceil(jnp.log2(jnp.maximum(peak, 2.0**-100)))
        power = jnp.broadcast_to(power, (1, width))
        out[n * width : (n + 1) * width, :] = block * jnp.exp2(TOP - power)
        codes = jnp.where(at == n, jnp.broadcast_to(power, (16, width)), codes)
    out[count * width :, :] = codes


def decode(ref, n, width, count):
    power = ref[count * width :, :][n : n + 1, :]
    return ref[pl.ds(n * width, width), :] * jnp.exp2(power - TOP)


def own_kernel(ints, mine, other, out, *, aux_count, npart, width):
    _, z, c = place()
    per_dev = mine.shape[0]
    for s in range(per_dev):
        for src, core in ((mine, c), (other, 1 - c)):
            at = per_dev * core + s
            out[at] = partial_residual(ints, aux_count * z + at, src[s], npart, width)


def far_kernel(ints, *refs, aux_count, distances, npart, width):
    a, z, c = place()
    outs, held = refs[aux_count:-1], refs[-1]
    for n, d in enumerate(distances):
        for e in range(aux_count):
            at = chip_slot(a ^ e, c)
            held[n, at] = partial_residual(ints, aux_count * (z ^ d) + at, refs[e][n], npart, width)
        encode(held.at[n], outs[n])


def join_kernel(*refs):
    *ins, _, out = refs
    for n, ref in enumerate(ins):
        out[n] = ref[...]


def sum_kernel(own, *refs):
    *ins, total, coded = refs
    count, width, _ = own.shape
    for n in range(count):
        value = own[n]
        for ref in ins:
            value = value + decode(ref, n, width, count)
        total[n] = value
    encode(total, coded)


def sum_split_kernel(own, *refs):
    *ins, keep, give, held = refs
    core = lax.axis_index("tile") % 2
    count, width, _ = own.shape
    per_dev = keep.shape[0]
    for n in range(count):
        value = own[n]
        for ref in ins:
            value = value + decode(ref, n, width, count)
        held[n] = value
    for s in range(per_dev):
        keep[s] = held[per_dev * core + s]
        give[s] = held[per_dev * (1 - core) + s]


def place_kernel(keep, got, out):
    core = lax.axis_index("tile") % 2
    out[core] = keep[...]
    out[1 - core] = got[...]


def per_device(integrals, coefficients, owned_tiles, pair_list, amplitudes):
    aux_count, tile_count = lax.axis_size("aux"), lax.axis_size("tile")
    chips = tile_count // 2
    rows, occ, ao = integrals.shape
    virt = coefficients.shape[1]
    batch_occ = occ // NB
    _, per_dev, npart, width, _ = amplitudes.shape
    slots = owned_tiles.shape[1]
    assert aux_count == 2 * per_dev and per_dev == 2

    def exchange(x, target):
        perm = []
        for a in range(aux_count):
            for z in range(chips):
                for c in range(2):
                    a2, z2, c2 = target(a, z, c)
                    perm.append((a * tile_count + 2 * z + c, a2 * tile_count + 2 * z2 + c2))
        return lax.ppermute(x, AXES, perm)

    def swap(x):
        return exchange(x, lambda a, z, c: (a, z, 1 - c))

    def round_plane(x):
        return [exchange(x, lambda a, z, c, e=e: (a ^ e, z, c)) for e in range(1, aux_count)]

    parts = 4
    cols = virt // parts
    padded = -(-rows // 16) * 16

    msg_rows = npart * width + 16
    msg = shape((msg_rows, width), BF16)
    pair = shape((per_dev, msg_rows, width), BF16)
    zmsg, mine, other = call(
        functools.partial(pack_kernel, npart=npart, width=width), [msg, pair, pair], [SMEM, VMEM], 12,
            )(pair_list, amplitudes)
    along = [exchange(zmsg, lambda a, z, c, d=d: (a, z ^ d, c ^ (a % 2))) for d in range(1, chips)]
    other = swap(other)
    batches = [range(1, chips - 1), range(chips - 1, chips)]
    far = []

    half = shape((batch_occ, padded, cols), BF16)
    acc = pltpu.VMEM((cols // 128, rows * occ, 128), F32)
    y_mine, y_other = [], []
    after = [zmsg]
    for n in range(parts):
        if n == 0:
            got, send, c = call(
                functools.partial(first_half_kernel, batch_occ=batch_occ),
                [half, half, shape(coefficients.shape, BF16)],
                [VMEM, HBM, ANY], 28, flops=HALF_FLOPS, scratch_shapes=[acc, pltpu.SemaphoreType.DMA((parts,))],
            )(integrals, coefficients, *after)
        else:
            got, send = call(
                functools.partial(half_kernel, batch_occ=batch_occ, start=n * cols),
                [half, half], [VMEM, VMEM] + [ANY] * len(after), 12, flops=HALF_FLOPS, scratch_shapes=[acc],
            )(integrals, c, *after)
        y_mine.append(got)
        y_other.append(swap(send))
        after = [got]
        if n == 2:
            after = far[0][1:]
        if n < len(batches):
            distances = batches[n]
            joined = call(
                join_kernel, shape((len(distances), msg_rows, width), BF16), [VMEM] * len(distances) + [ANY], 12
            )(*[along[d - 1] for d in distances], got)
            far.append([joined] + round_plane(joined))
            after = [joined]

    ints_shape = shape((slots, BAND, width, width), F32)
    tiles_shape = (2 * padded, (slots + BAND - 1) * width)
    ints = call(
        functools.partial(pair_kernel, parts=parts, width=width), ints_shape, [SMEM] + [VMEM] * (2 * parts),
        8 + 4 * slots * BAND * width * width // MIB + 2 * tiles_shape[0] * tiles_shape[1] // MIB,
        scratch_shapes=[pltpu.VMEM(tiles_shape, BF16), pltpu.SMEM((slots,), jnp.int32)],
    )(owned_tiles, *y_mine, *y_other)

    chip_part = shape((aux_count, width, width), F32)
    sizes = dict(aux_count=aux_count, npart=npart, width=width)
    got = [call(functools.partial(own_kernel, **sizes), chip_part, [VMEM] * 3, 12)(ints, mine, other)]
    coded = shape((aux_count * width + 16, width), F32)
    for distances, amps in zip(batches, far):
        shares = call(
            functools.partial(far_kernel, distances=distances, **sizes),
            [coded] * len(distances), [VMEM] * (1 + aux_count), 16,
            scratch_shapes=[pltpu.VMEM((len(distances),) + chip_part.shape, F32)],
        )(ints, *amps)
        for d, share in zip(distances, shares):
            got.append(exchange(share.astype(F16), lambda a, z, c, d=d: (a, z ^ d, c)).astype(F32))
    column, share = call(sum_kernel, [chip_part, coded], [VMEM] * chips, 12)(*got)

    core_part = shape((per_dev, width, width), F32)
    got = [x.astype(F32) for x in round_plane(share.astype(F16))]
    keep, give = call(
        sum_split_kernel, [core_part] * 2, [VMEM] * aux_count, 12, scratch_shapes=[pltpu.VMEM(chip_part.shape, F32)]
    )(column, *got)
    return call(place_kernel, shape((NB, per_dev, width, width), F32), [VMEM] * 2, 8)(keep, swap(give))


def solution(mesh):
    in_specs = (
        P(("aux", "tile"), None, None),
        P(),
        P(),
        P(None, "tile", None),
        P(None, "tile", None, None, None),
    )
    out_specs = P(None, "tile", None, None)
    return jax.shard_map(
        per_device, mesh=mesh, in_specs=in_specs, out_specs=out_specs, check_vma=False
    )
```

```python
import functools

import jax
import jax.numpy as jnp
from jax import lax
from jax.experimental import pallas as pl
from jax.experimental.pallas import tpu as pltpu
from jax.sharding import PartitionSpec as P

NB = 2
BAND = 5
REACH = BAND // 2
PARTS = 8
STEPS = (2, 2, 3, 1)
JOIN_AFTER = (0, 2)
ORDER = {
    "j0": ("C0",),
    "C1": ("j0",),
    "C2": ("C1",),
    "j1": ("C2",),
    "C3": ("x00", "x01", "x02", "j1"),
    "far1": ("far0",),
    "own": ("far1",),
}
MIB = 2**20
AXES = ("aux", "tile")
VMEM = pl.BlockSpec(memory_space=pltpu.VMEM)
SMEM = pl.BlockSpec(memory_space=pltpu.SMEM)
ANY = pl.BlockSpec(memory_space=pl.ANY)
HBM = pl.BlockSpec(memory_space=pltpu.HBM)
F32, BF16, F16 = jnp.float32, jnp.bfloat16, jnp.float16
TOP = 15.0


def shape(dims, dtype):
    return jax.ShapeDtypeStruct(tuple(dims), dtype)


def place():
    t = lax.axis_index("tile")
    return lax.axis_index("aux"), t // 2, t % 2


def chip_slot(a, batch):
    return 2 * ((a % 2) ^ batch) + a // 2


def call(name, kernel, outs, specs, limit, **kw):
    return pl.pallas_call(
        kernel, name=name, in_specs=specs, out_specs=jax.tree.map(lambda _: VMEM, outs), out_shape=outs,
        compiler_params=pltpu.CompilerParams(vmem_limit_bytes=limit * MIB),
        cost_estimate=pl.CostEstimate(flops=10**6, bytes_accessed=10**5, transcendentals=0), **kw,
    )


def pack_kernel(pairs, amps, zmsg, mine, other, token, *, npart, width):
    token[...] = jnp.zeros_like(token)
    a, z, c = place()
    per_dev = amps.shape[1]
    first = lax.axis_index("tile") * per_dev

    def pack(batch, s, dst):
        offsets, live, seen = [], [], [jnp.int32(0)] * BAND
        for k in range(npart):
            p = pairs[batch, s, k]
            o = p - (first + s) + REACH
            ok = p >= 0
            offsets.append(o)
            live.append(ok)
            for n in range(BAND):
                seen[n] = jnp.where(ok & (o == n), 1, seen[n])
        m = jnp.int32(BAND - 1)
        for n in reversed(range(BAND)):
            m = jnp.where(seen[n] == 0, n, m)
        for j in range(npart):
            want = j + jnp.where(j >= m, 1, 0)
            found, at = jnp.int32(0), jnp.int32(0)
            for k in range(npart):
                hit = live[k] & (offsets[k] == want)
                found = jnp.where(hit, 1, found)
                at = jnp.where(hit, k, at)
            block = amps[batch, s, at]
            dst[pl.ds(j * width, width), :] = jnp.where(found == 1, block, jnp.zeros_like(block))
        code = jnp.full((16, width), m.astype(F32), F32)
        dst[pl.ds(npart * width, 16), :] = code.astype(BF16)

    pack(c ^ (a % 2), a // 2, zmsg)
    for s in range(per_dev):
        pack(c, s, mine.at[s])
        pack(1 - c, s, other.at[s])


def half_columns(x_ref, c_ref, start, at, count, mine, other, acc, batch_occ):
    core = lax.axis_index("tile") % 2
    rows, occ, ao = x_ref.shape
    padded = mine.shape[1]
    prod = jnp.dot(
        x_ref[...].reshape(rows * occ, ao), c_ref[:, start : start + count], preferred_element_type=F32
    )
    for n in range(count // 128):
        acc[n] = prod[:, n * 128 : (n + 1) * 128]
    for i in range(batch_occ):
        for n in range(count // 128):
            lanes = slice(at + n * 128, at + (n + 1) * 128)
            for dst, b in ((mine, core), (other, 1 - core)):
                part = acc[n, pl.ds(b * batch_occ + i, rows, stride=occ), :]
                dst[i, :rows, lanes] = part.astype(BF16)
    for dst in (mine, other):
        dst[:, rows:, at : at + count] = jnp.zeros((batch_occ, padded - rows, count), BF16)


def first_half_kernel(x_ref, c_hbm, _, mine, other, c_ref, acc, sems, *, batch_occ):
    piece = mine.shape[2]
    get_c = [
        pltpu.make_async_copy(
            c_hbm.at[:, pl.ds(n, piece)], c_ref.at[:, pl.ds(n, piece)], sems.at[n // piece]
        )
        for n in range(0, c_ref.shape[1], piece)
    ]
    for copy in get_c:
        copy.start()
    get_c[0].wait()
    half_columns(x_ref, c_ref, 0, 0, piece, mine, other, acc, batch_occ)
    for copy in get_c[1:]:
        copy.wait()


def half_kernel(x_ref, c_ref, *rest, batch_occ, start):
    mine, other, acc = rest[-3:]
    most = acc.shape[0] * 128
    cols = mine.shape[2]
    for n in range(0, cols, most):
        half_columns(x_ref, c_ref, start + n, n, min(most, cols - n), mine, other, acc, batch_occ)


def order_kernel(owned, *refs, parts, width):
    core = lax.axis_index("tile") % 2
    slots = owned.shape[1]
    y_mine, y_other, (tiles, place_of) = refs[:parts], refs[parts : 2 * parts], refs[-2:]
    batch_occ, padded, _ = y_mine[0].shape
    virt_tiles = slots // batch_occ
    for s in range(slots):
        place_of[owned[core, s]] = s + REACH
    for n in (0, 1, slots + REACH, slots + REACH + 1):
        tiles[:, n * width : (n + 1) * width] = jnp.zeros((2 * padded, width), BF16)
    for i in range(batch_occ):
        first = 0
        for h in range(parts):
            count = y_mine[h].shape[2] // width
            for n in range(count):
                ident = i * virt_tiles + first + n
                lanes = pl.ds(pl.multiple_of(place_of[ident] * width, width), width)
                for src, group in enumerate((y_mine, y_other)):
                    rows = slice(src * padded, (src + 1) * padded)
                    tiles[rows, lanes] = group[h][i, :, n * width : (n + 1) * width]
            first += count


def pair_ints(tiles, first, ints):
    count, _, width, _ = ints.shape
    for t in range(0, count, 2):
        at = pl.multiple_of((first + t) * width, width)
        left = tiles[:, pl.ds(at + REACH * width, 2 * width)]
        right = tiles[:, pl.ds(at, (2 + 2 * REACH) * width)]
        total = lax.dot_general(left, right, (((0,), (0,)), ((), ())), preferred_element_type=F32)
        for u in range(2):
            for o in range(BAND):
                ints[t + u, o] = total[u * width : (u + 1) * width, (u + o) * width : (u + o + 1) * width]


def partial_residual(ints, slot, amp, npart, width):
    rows = amp[: npart * width]
    m = amp[npart * width :].astype(F32)[:1, :]
    picked = [jnp.where(m > j, ints[slot, j], ints[slot, j + 1]) for j in range(npart)]
    picked = jnp.concatenate(picked, axis=1)
    high = picked.astype(BF16)
    low = (picked - high.astype(F32)).astype(BF16)
    return jnp.dot(high, rows, preferred_element_type=F32) + jnp.dot(low, rows, preferred_element_type=F32)


def encode(blocks, out):
    count, width, _ = blocks.shape
    at = lax.broadcasted_iota(jnp.int32, (16, width), 0)
    codes = jnp.zeros((16, width), F32)
    for n in range(count):
        block = blocks[n]
        peak = jnp.max(jnp.abs(block), axis=0, keepdims=True)
        peak = jnp.max(peak, axis=1, keepdims=True)
        power = jnp.ceil(jnp.log2(jnp.maximum(peak, 2.0**-100)))
        power = jnp.broadcast_to(power, (1, width))
        out[n * width : (n + 1) * width, :] = block * jnp.exp2(TOP - power)
        codes = jnp.where(at == n, jnp.broadcast_to(power, (16, width)), codes)
    out[count * width :, :] = codes


def decode(ref, n, width, count):
    power = ref[count * width :, :][n : n + 1, :]
    return ref[pl.ds(n * width, width), :] * jnp.exp2(power - TOP)


def own_kernel(tiles, mine, other, *refs, aux_count, npart, width):
    out, ints = refs[-2:]
    _, z, c = place()
    per_dev = mine.shape[0]
    pair_ints(tiles, aux_count * z, ints)
    for s in range(per_dev):
        for src, core in ((mine, c), (other, 1 - c)):
            at = per_dev * core + s
            out[at] = partial_residual(ints, at, src[s], npart, width)


def far_kernel(tiles, *refs, aux_count, distances, npart, width):
    a, z, c = place()
    outs, (held, ints) = refs[-2 - len(distances) : -2], refs[-2:]
    for n, d in enumerate(distances):
        pair_ints(tiles, aux_count * (z ^ d), ints)
        for e in range(aux_count):
            at = chip_slot(a ^ e, c)
            held[at] = partial_residual(ints, at, refs[e][n], npart, width)
        encode(held, outs[n])


def join_kernel(*refs):
    out = refs[-1]
    for n in range(out.shape[0]):
        out[n] = refs[n][...]


def sum_kernel(own, *refs):
    *ins, total, coded = refs
    count, width, _ = own.shape
    for n in range(count):
        value = own[n]
        for ref in ins:
            value = value + decode(ref, n, width, count)
        total[n] = value
    encode(total, coded)


def sum_split_kernel(own, *refs):
    *ins, keep, give, held = refs
    core = lax.axis_index("tile") % 2
    count, width, _ = own.shape
    per_dev = keep.shape[0]
    for n in range(count):
        value = own[n]
        for ref in ins:
            value = value + decode(ref, n, width, count)
        held[n] = value
    for s in range(per_dev):
        keep[s] = held[per_dev * core + s]
        give[s] = held[per_dev * (1 - core) + s]


def place_kernel(keep, got, out):
    core = lax.axis_index("tile") % 2
    out[core] = keep[...]
    out[1 - core] = got[...]


def per_device(integrals, coefficients, owned_tiles, pair_list, amplitudes):
    aux_count, tile_count = lax.axis_size("aux"), lax.axis_size("tile")
    chips = tile_count // 2
    rows, occ, ao = integrals.shape
    virt = coefficients.shape[1]
    batch_occ = occ // NB
    _, per_dev, npart, width, _ = amplitudes.shape
    slots = owned_tiles.shape[1]
    assert aux_count == 2 * per_dev and per_dev == 2

    def exchange(x, target):
        perm = []
        for a in range(aux_count):
            for z in range(chips):
                for c in range(2):
                    a2, z2, c2 = target(a, z, c)
                    perm.append((a * tile_count + 2 * z + c, a2 * tile_count + 2 * z2 + c2))
        return lax.ppermute(x, AXES, perm)

    def swap(x):
        return exchange(x, lambda a, z, c: (a, z, 1 - c))

    def round_plane(x):
        return [exchange(x, lambda a, z, c, e=e: (a ^ e, z, c)) for e in range(1, aux_count)]

    cols = virt // PARTS
    padded = -(-rows // 16) * 16

    msg_rows = npart * width + 16
    msg = shape((msg_rows, width), BF16)
    pair = shape((per_dev, msg_rows, width), BF16)
    zmsg, mine, other, token = call(
        "pack", functools.partial(pack_kernel, npart=npart, width=width),
        [msg, pair, pair, shape((8, 128), F32)], [SMEM, VMEM], 12,
    )(pair_list, amplitudes)
    along = [exchange(zmsg, lambda a, z, c, d=d: (a, z ^ d, c ^ (a % 2))) for d in range(1, chips)]
    other = swap(other)
    marks = {"z": zmsg, "o": other}

    def deps_for(name):
        return [marks[key] for key in ORDER.get(name, ())]

    batches = [range(chips - 2, 0, -1), range(chips - 1, chips)]
    far = []

    first_cols = STEPS[0] * cols
    acc = pltpu.VMEM((first_cols // 128, rows * occ, 128), F32)
    y_mine, y_other = [], []
    start = 0
    for step, count in enumerate(STEPS):
        half = shape((batch_occ, padded, count * cols), BF16)
        after = deps_for("C%d" % step)
        if step == 0:
            got, send, c = call(
                "half0", functools.partial(first_half_kernel, batch_occ=batch_occ),
                [half, half, shape(coefficients.shape, BF16)],
                [VMEM, HBM, ANY], 28, scratch_shapes=[acc, pltpu.SemaphoreType.DMA((virt // first_cols,))],
            )(integrals, coefficients, token)
        else:
            got, send = call(
                "half%d" % step, functools.partial(half_kernel, batch_occ=batch_occ, start=start * cols),
                [half, half], [VMEM, VMEM] + [ANY] * len(after), 12, scratch_shapes=[acc],
            )(integrals, c, *after)
        start += count
        y_mine.append(got)
        y_other.append(swap(send))
        marks["C%d" % step] = got
        marks["y%d" % step] = y_other[-1]
        if step in JOIN_AFTER:
            distances = batches[JOIN_AFTER.index(step)]
            after = deps_for("j%d" % len(far))
            joined = call(
                "join%d" % len(far), join_kernel, shape((len(distances), msg_rows, width), BF16),
                [VMEM] * len(distances) + [ANY] * len(after), 12
            )(*[along[d - 1] for d in distances], *after)
            marks["j%d" % len(far)] = joined
            around = round_plane(joined)
            for e, x in enumerate(around):
                marks["x%d%d" % (len(far), e)] = x
            far.append([joined] + around)

    after = deps_for("T")
    tiles = call(
        "order", functools.partial(order_kernel, parts=len(STEPS), width=width),
        shape((2 * padded, (slots + BAND - 1) * width), BF16),
        [SMEM] + [VMEM] * (2 * len(STEPS)) + [ANY] * len(after), 12,
        scratch_shapes=[pltpu.SMEM((slots,), jnp.int32)],
    )(owned_tiles, *y_mine, *y_other, *after)

    chip_part = shape((aux_count, width, width), F32)
    coded = shape((aux_count * width + 16, width), F32)
    ints = pltpu.VMEM((aux_count, BAND, width, width), F32)
    sizes = dict(aux_count=aux_count, npart=npart, width=width)
    got = []
    for n, (distances, amps) in enumerate(zip(batches, far)):
        after = deps_for("far%d" % n)
        shares = call(
            "far%d" % n, functools.partial(far_kernel, distances=distances, **sizes),
            [coded] * len(distances), [VMEM] * (1 + aux_count) + [ANY] * len(after), 16,
            scratch_shapes=[pltpu.VMEM(chip_part.shape, F32), ints],
        )(tiles, *amps, *after)
        marks["far%d" % n] = shares[0]
        for d, share in zip(distances, shares):
            got.append(exchange(share.astype(F16), lambda a, z, c, d=d: (a, z ^ d, c)).astype(F32))
    after = deps_for("own")
    own = call(
        "own", functools.partial(own_kernel, **sizes), chip_part, [VMEM] * 3 + [ANY] * len(after), 12,
        scratch_shapes=[ints],
    )(tiles, mine, other, *after)
    got = [own] + got
    column, share = call("along", sum_kernel, [chip_part, coded], [VMEM] * chips, 12)(*got)

    core_part = shape((per_dev, width, width), F32)
    got = [x.astype(F32) for x in round_plane(share.astype(F16))]
    keep, give = call(
        "around", sum_split_kernel, [core_part] * 2, [VMEM] * aux_count, 12,
        scratch_shapes=[pltpu.VMEM(chip_part.shape, F32)],
    )(column, *got)
    return call("place", place_kernel, shape((NB, per_dev, width, width), F32), [VMEM] * 2, 8)(keep, swap(give))


def solution(mesh):
    in_specs = (
        P(("aux", "tile"), None, None),
        P(),
        P(),
        P(None, "tile", None),
        P(None, "tile", None, None, None),
    )
    out_specs = P(None, "tile", None, None)
    return jax.shard_map(
        per_device, mesh=mesh, in_specs=in_specs, out_specs=out_specs, check_vma=False
    )
```

```python
import functools

import jax
import jax.numpy as jnp
from jax import lax
from jax.experimental import pallas as pl
from jax.experimental.pallas import tpu as pltpu
from jax.sharding import PartitionSpec as P

NB = 2
BAND = 5
REACH = BAND // 2
PARTS = 8
STEPS = (2, 2, 3, 1)
JOIN_AFTER = (0, 2)
ORDER = {
    "j0": ("C0",),
    "C1": ("j0",),
    "C2": ("C1",),
    "j1": ("C2",),
    "C3": ("x00", "x01", "x02", "j1"),
    "far1": ("far0",),
    "own": ("far1",),
}
MIB = 2**20
AXES = ("aux", "tile")
VMEM = pl.BlockSpec(memory_space=pltpu.VMEM)
SMEM = pl.BlockSpec(memory_space=pltpu.SMEM)
ANY = pl.BlockSpec(memory_space=pl.ANY)
HBM = pl.BlockSpec(memory_space=pltpu.HBM)
F32, BF16, F16 = jnp.float32, jnp.bfloat16, jnp.float16
TOP = 15.0


def shape(dims, dtype):
    return jax.ShapeDtypeStruct(tuple(dims), dtype)


def place():
    t = lax.axis_index("tile")
    return lax.axis_index("aux"), t // 2, t % 2


def chip_slot(a, batch):
    return 2 * ((a % 2) ^ batch) + a // 2


def call(name, kernel, outs, specs, limit, **kw):
    return pl.pallas_call(
        kernel, name=name, in_specs=specs, out_specs=jax.tree.map(lambda _: VMEM, outs), out_shape=outs,
        compiler_params=pltpu.CompilerParams(vmem_limit_bytes=limit * MIB),
        cost_estimate=pl.CostEstimate(flops=10**6, bytes_accessed=10**5, transcendentals=0), **kw,
    )


def pack_kernel(pairs, amps, zmsg, mine, other, token, *, npart, width):
    token[...] = jnp.zeros_like(token)
    a, z, c = place()
    per_dev = amps.shape[1]
    first = lax.axis_index("tile") * per_dev

    def pack(batch, s, dst):
        offsets, live, seen = [], [], [jnp.int32(0)] * BAND
        for k in range(npart):
            p = pairs[batch, s, k]
            o = p - (first + s) + REACH
            ok = p >= 0
            offsets.append(o)
            live.append(ok)
            for n in range(BAND):
                seen[n] = jnp.where(ok & (o == n), 1, seen[n])
        m = jnp.int32(BAND - 1)
        for n in reversed(range(BAND)):
            m = jnp.where(seen[n] == 0, n, m)
        for j in range(npart):
            want = j + jnp.where(j >= m, 1, 0)
            found, at = jnp.int32(0), jnp.int32(0)
            for k in range(npart):
                hit = live[k] & (offsets[k] == want)
                found = jnp.where(hit, 1, found)
                at = jnp.where(hit, k, at)
            block = amps[batch, s, at]
            dst[pl.ds(j * width, width), :] = jnp.where(found == 1, block, jnp.zeros_like(block))
        code = jnp.full((16, width), m.astype(F32), F32)
        dst[pl.ds(npart * width, 16), :] = code.astype(BF16)

    pack(c ^ (a % 2), a // 2, zmsg)
    for s in range(per_dev):
        pack(c, s, mine.at[s])
        pack(1 - c, s, other.at[s])


def half_columns(x_ref, c_ref, start, at, count, mine, other, acc, batch_occ):
    core = lax.axis_index("tile") % 2
    rows, occ, ao = x_ref.shape
    padded = mine.shape[1]
    prod = jnp.dot(
        x_ref[...].reshape(rows * occ, ao), c_ref[:, start : start + count], preferred_element_type=F32
    )
    for n in range(count // 128):
        acc[n, : rows * occ, :] = prod[:, n * 128 : (n + 1) * 128]
    for i in range(batch_occ):
        for n in range(count // 128):
            lanes = slice(at + n * 128, at + (n + 1) * 128)
            for dst, b in ((mine, core), (other, 1 - core)):
                part = acc[n, pl.ds(b * batch_occ + i, rows, stride=occ), :]
                dst[i, :rows, lanes] = part.astype(BF16)
    for dst in (mine, other):
        dst[:, rows:, at : at + count] = jnp.zeros((batch_occ, padded - rows, count), BF16)


def first_half_kernel(x_ref, c_hbm, _, mine, other, c_ref, acc, sems, *, batch_occ):
    piece = mine.shape[2]
    get_c = [
        pltpu.make_async_copy(
            c_hbm.at[:, pl.ds(n, piece)], c_ref.at[:, pl.ds(n, piece)], sems.at[n // piece]
        )
        for n in range(0, c_ref.shape[1], piece)
    ]
    for copy in get_c:
        copy.start()
    get_c[0].wait()
    half_columns(x_ref, c_ref, 0, 0, piece, mine, other, acc, batch_occ)
    for copy in get_c[1:]:
        copy.wait()


def half_kernel(x_ref, c_ref, *rest, batch_occ, start):
    mine, other, acc = rest[-3:]
    most = acc.shape[0] * 128
    cols = mine.shape[2]
    for n in range(0, cols, most):
        half_columns(x_ref, c_ref, start + n, n, min(most, cols - n), mine, other, acc, batch_occ)


def order_kernel(owned, *refs, parts, width):
    core = lax.axis_index("tile") % 2
    slots = owned.shape[1]
    y_mine, y_other, (tiles, place_of) = refs[:parts], refs[parts : 2 * parts], refs[-2:]
    batch_occ, padded, _ = y_mine[0].shape
    virt_tiles = slots // batch_occ
    for s in range(slots):
        place_of[owned[core, s]] = s + REACH
    for n in (0, 1, slots + REACH, slots + REACH + 1):
        tiles[:, n * width : (n + 1) * width] = jnp.zeros((2 * padded, width), BF16)
    for i in range(batch_occ):
        first = 0
        for h in range(parts):
            count = y_mine[h].shape[2] // width
            for n in range(count):
                ident = i * virt_tiles + first + n
                lanes = pl.ds(pl.multiple_of(place_of[ident] * width, width), width)
                for src, group in enumerate((y_mine, y_other)):
                    rows = slice(src * padded, (src + 1) * padded)
                    tiles[rows, lanes] = group[h][i, :, n * width : (n + 1) * width]
            first += count


def pair_ints(tiles, first, ints):
    count, _, width, _ = ints.shape
    for t in range(0, count, 2):
        at = pl.multiple_of((first + t) * width, width)
        left = tiles[:, pl.ds(at + REACH * width, 2 * width)]
        right = tiles[:, pl.ds(at, (2 + 2 * REACH) * width)]
        total = lax.dot_general(left, right, (((0,), (0,)), ((), ())), preferred_element_type=F32)
        for u in range(2):
            for o in range(BAND):
                ints[t + u, o] = total[u * width : (u + 1) * width, (u + o) * width : (u + o + 1) * width]


def partial_residual(ints, slot, amp, npart, width):
    rows = amp[: npart * width]
    m = amp[npart * width :].astype(F32)[:1, :]
    picked = [jnp.where(m > j, ints[slot, j], ints[slot, j + 1]) for j in range(npart)]
    picked = jnp.concatenate(picked, axis=1)
    high = picked.astype(BF16)
    low = (picked - high.astype(F32)).astype(BF16)
    return jnp.dot(high, rows, preferred_element_type=F32) + jnp.dot(low, rows, preferred_element_type=F32)


def encode(blocks, out):
    count, width, _ = blocks.shape
    at = lax.broadcasted_iota(jnp.int32, (16, width), 0)
    codes = jnp.zeros((16, width), F32)
    for n in range(count):
        block = blocks[n]
        peak = jnp.max(jnp.abs(block), axis=0, keepdims=True)
        peak = jnp.max(peak, axis=1, keepdims=True)
        power = jnp.ceil(jnp.log2(jnp.maximum(peak, 2.0**-100)))
        power = jnp.broadcast_to(power, (1, width))
        out[n * width : (n + 1) * width, :] = block * jnp.exp2(TOP - power)
        codes = jnp.where(at == n, jnp.broadcast_to(power, (16, width)), codes)
    out[count * width :, :] = codes


def decode(ref, n, width, count):
    power = ref[count * width :, :][n : n + 1, :]
    return ref[pl.ds(n * width, width), :] * jnp.exp2(power - TOP)


def own_kernel(tiles, mine, other, *refs, aux_count, npart, width):
    out, ints = refs[-2:]
    _, z, c = place()
    per_dev = mine.shape[0]
    pair_ints(tiles, aux_count * z, ints)
    for s in range(per_dev):
        for src, core in ((mine, c), (other, 1 - c)):
            at = per_dev * core + s
            out[at] = partial_residual(ints, at, src[s], npart, width)


def far_kernel(tiles, *refs, aux_count, distances, npart, width):
    a, z, c = place()
    outs, (held, ints) = refs[-2 - len(distances) : -2], refs[-2:]
    for n, d in enumerate(distances):
        pair_ints(tiles, aux_count * (z ^ d), ints)
        for e in range(aux_count):
            at = chip_slot(a ^ e, c)
            held[at] = partial_residual(ints, at, refs[e][n], npart, width)
        encode(held, outs[n])


def join_kernel(*refs):
    out = refs[-1]
    for n in range(out.shape[0]):
        out[n] = refs[n][...]


def sum_kernel(own, *refs):
    *ins, total, coded = refs
    count, width, _ = own.shape
    for n in range(count):
        value = own[n]
        for ref in ins:
            value = value + decode(ref, n, width, count)
        total[n] = value
    encode(total, coded)


def sum_split_kernel(own, *refs):
    *ins, keep, give, held = refs
    core = lax.axis_index("tile") % 2
    count, width, _ = own.shape
    per_dev = keep.shape[0]
    for n in range(count):
        value = own[n]
        for ref in ins:
            value = value + decode(ref, n, width, count)
        held[n] = value
    for s in range(per_dev):
        keep[s] = held[per_dev * core + s]
        give[s] = held[per_dev * (1 - core) + s]


def place_kernel(keep, got, out):
    core = lax.axis_index("tile") % 2
    out[core] = keep[...]
    out[1 - core] = got[...]


def per_device(integrals, coefficients, owned_tiles, pair_list, amplitudes):
    aux_count, tile_count = lax.axis_size("aux"), lax.axis_size("tile")
    chips = tile_count // 2
    rows, occ, ao = integrals.shape
    virt = coefficients.shape[1]
    batch_occ = occ // NB
    _, per_dev, npart, width, _ = amplitudes.shape
    slots = owned_tiles.shape[1]
    assert aux_count == 2 * per_dev and per_dev == 2

    def exchange(x, target):
        perm = []
        for a in range(aux_count):
            for z in range(chips):
                for c in range(2):
                    a2, z2, c2 = target(a, z, c)
                    perm.append((a * tile_count + 2 * z + c, a2 * tile_count + 2 * z2 + c2))
        return lax.ppermute(x, AXES, perm)

    def swap(x):
        return exchange(x, lambda a, z, c: (a, z, 1 - c))

    def round_plane(x):
        return [exchange(x, lambda a, z, c, e=e: (a ^ e, z, c)) for e in range(1, aux_count)]

    cols = virt // PARTS
    padded = -(-rows // 16) * 16

    msg_rows = npart * width + 16
    msg = shape((msg_rows, width), BF16)
    pair = shape((per_dev, msg_rows, width), BF16)
    zmsg, mine, other, token = call(
        "pack", functools.partial(pack_kernel, npart=npart, width=width),
        [msg, pair, pair, shape((8, 128), F32)], [SMEM, VMEM], 12,
    )(pair_list, amplitudes)
    along = [exchange(zmsg, lambda a, z, c, d=d: (a, z ^ d, c ^ (a % 2))) for d in range(1, chips)]
    other = swap(other)
    marks = {"z": zmsg, "o": other}

    def deps_for(name):
        return [marks[key] for key in ORDER.get(name, ())]

    batches = [range(chips - 2, 0, -1), range(chips - 1, chips)]
    far = []

    first_cols = STEPS[0] * cols
    acc = pltpu.VMEM((first_cols // 128, (-(-rows // 8) * 8 + 8) * occ, 128), F32)
    y_mine, y_other = [], []
    start = 0
    for step, count in enumerate(STEPS):
        half = shape((batch_occ, padded, count * cols), BF16)
        after = deps_for("C%d" % step)
        if step == 0:
            got, send, c = call(
                "half0", functools.partial(first_half_kernel, batch_occ=batch_occ),
                [half, half, shape(coefficients.shape, BF16)],
                [VMEM, HBM, ANY], 28, scratch_shapes=[acc, pltpu.SemaphoreType.DMA((virt // first_cols,))],
            )(integrals, coefficients, token)
        else:
            got, send = call(
                "half%d" % step, functools.partial(half_kernel, batch_occ=batch_occ, start=start * cols),
                [half, half], [VMEM, VMEM] + [ANY] * len(after), 12, scratch_shapes=[acc],
            )(integrals, c, *after)
        start += count
        y_mine.append(got)
        y_other.append(swap(send))
        marks["C%d" % step] = got
        marks["y%d" % step] = y_other[-1]
        if step in JOIN_AFTER:
            distances = batches[JOIN_AFTER.index(step)]
            after = deps_for("j%d" % len(far))
            joined = call(
                "join%d" % len(far), join_kernel, shape((len(distances), msg_rows, width), BF16),
                [VMEM] * len(distances) + [ANY] * len(after), 12
            )(*[along[d - 1] for d in distances], *after)
            marks["j%d" % len(far)] = joined
            around = round_plane(joined)
            for e, x in enumerate(around):
                marks["x%d%d" % (len(far), e)] = x
            far.append([joined] + around)

    after = deps_for("T")
    tiles = call(
        "order", functools.partial(order_kernel, parts=len(STEPS), width=width),
        shape((2 * padded, (slots + BAND - 1) * width), BF16),
        [SMEM] + [VMEM] * (2 * len(STEPS)) + [ANY] * len(after), 12,
        scratch_shapes=[pltpu.SMEM((slots,), jnp.int32)],
    )(owned_tiles, *y_mine, *y_other, *after)

    chip_part = shape((aux_count, width, width), F32)
    coded = shape((aux_count * width + 16, width), F32)
    ints = pltpu.VMEM((aux_count, BAND, width, width), F32)
    sizes = dict(aux_count=aux_count, npart=npart, width=width)
    got = []
    for n, (distances, amps) in enumerate(zip(batches, far)):
        after = deps_for("far%d" % n)
        shares = call(
            "far%d" % n, functools.partial(far_kernel, distances=distances, **sizes),
            [coded] * len(distances), [VMEM] * (1 + aux_count) + [ANY] * len(after), 16,
            scratch_shapes=[pltpu.VMEM(chip_part.shape, F32), ints],
        )(tiles, *amps, *after)
        marks["far%d" % n] = shares[0]
        for d, share in zip(distances, shares):
            got.append(exchange(share.astype(F16), lambda a, z, c, d=d: (a, z ^ d, c)).astype(F32))
    after = deps_for("own")
    own = call(
        "own", functools.partial(own_kernel, **sizes), chip_part, [VMEM] * 3 + [ANY] * len(after), 12,
        scratch_shapes=[ints],
    )(tiles, mine, other, *after)
    got = [own] + got
    column, share = call("along", sum_kernel, [chip_part, coded], [VMEM] * chips, 12)(*got)

    core_part = shape((per_dev, width, width), F32)
    got = [x.astype(F32) for x in round_plane(share.astype(F16))]
    keep, give = call(
        "around", sum_split_kernel, [core_part] * 2, [VMEM] * aux_count, 12,
        scratch_shapes=[pltpu.VMEM(chip_part.shape, F32)],
    )(column, *got)
    return call("place", place_kernel, shape((NB, per_dev, width, width), F32), [VMEM] * 2, 8)(keep, swap(give))


def solution(mesh):
    in_specs = (
        P(("aux", "tile"), None, None),
        P(),
        P(),
        P(None, "tile", None),
        P(None, "tile", None, None, None),
    )
    out_specs = P(None, "tile", None, None)
    return jax.shard_map(
        per_device, mesh=mesh, in_specs=in_specs, out_specs=out_specs, check_vma=False
    )
```
